128 devices in a mesh: cmp: 32 (over y, z, x_lo), tgt: 4 (over x_hi, core).
Axes of the slice: x: 4 (x_hi: 2, x_lo: 2; x = x_hi * 2 + x_lo), y: 4, z: 4, core: 2. Of those that a mesh axis runs over, the one named last changes fastest.
Arguments:
- activity: bfloat16 [8192, 2048], P('cmp', 'tgt'), may hold values from -6 to 6
- drug_basis: bfloat16 [8192, 512], P('cmp'), as said below
- target_basis: bfloat16 [2048, 2048], P('tgt'), as said below
- drug_values: float32 [512], replicated, may hold values from 0.05 to 20
- target_values: float32 [2048], replicated, may hold values from 0.05 to 20
- ridge: float32 [1], replicated, may hold values from 0.5 to 2
Outputs:
- fitted: bfloat16 [8192, 2048], P('cmp', 'tgt')
- loo_residual: bfloat16 [8192, 2048], P('cmp', 'tgt')
The draws below stay inside these ranges and needn't reach their ends.
Inputs may be any that keep to these rules, and one draw needn't show every extreme that they name: Each row of drug_basis has squared entries summing to at most 0.5. Each row of target_basis has squared entries summing to at most 0.95.
All inputs are finite; a program needn't handle non-finite values.
Results may differ from the reference program's by a relative error of at most 0.002.
Values sent between devices are 32-bit elements; how exact they have to be, the bound alone decides.
No kernel may reach another device: no remote copies, remote signals or barrier semaphores. Data moves between devices by JAX's collectives and lax.ppermute only.
A program may use at most 64 MiB of HBM per device.

```python
import math
import jax
import jax.numpy as jnp
from jax import lax

R = 512
NT = 2048
NC = 8192


def banded_roots(key, rows, cols, width, total, entry_low, row_low):
    entry_key = jax.random.fold_in(key, 2)
    scale_key = jax.random.fold_in(key, 3)
    offset_key = jax.random.fold_in(key, 5)
    sign_key = jax.random.fold_in(key, 7)
    magnitudes = jax.random.uniform(entry_key, (rows, cols), jnp.float32, entry_low, 1.0)
    magnitudes = magnitudes * jax.random.uniform(scale_key, (rows, 1), jnp.float32, row_low, 1.0)
    offsets = jax.random.randint(offset_key, (rows, 1), 0, cols, dtype=jnp.int32)
    position = lax.broadcasted_iota(jnp.int32, (rows, cols), 1)
    inside = (position - offsets) % cols < width
    weights = jnp.where(inside, 0.85 / width, 0.15 / (cols - width)).astype(jnp.float32)
    signs = jax.random.rademacher(sign_key, (rows, cols), dtype=jnp.float32)
    return signs * jnp.sqrt(magnitudes * weights * total)


def draw_drug_basis(key, part):
    key = jax.random.fold_in(key, 1)
    width = max(R // 32, 4)
    values = banded_roots(key, NC, R, width, 0.5, 0.5, 1.0)
    return values.astype(jnp.bfloat16)


def draw_target_basis(key, part):
    key = jax.random.fold_in(key, 11)
    width = max(NT // 128, 4)
    values = banded_roots(key, NT, NT, width, 0.95, 0.5, 1.0)
    return values.astype(jnp.bfloat16)


def level_of(stream_key, shape, split, low, high):
    factor_of, own = 1.0, jax.random.fold_in(stream_key, 6)
    for dim, shards_of in split:
        draws = jnp.exp(jax.random.uniform(jax.random.fold_in(own, dim), (shards_of,), jnp.float32, low / len(split), high / len(split)))
        factor_of = factor_of * jnp.repeat(draws, shape[dim] // shards_of).reshape([-1 if axis == dim else 1 for axis in range(len(shape))])
    return factor_of


def gaussian(rng, shape, spread, bound, shards=(), kind=jnp.bfloat16):
    values = spread * jax.random.normal(rng, shape, jnp.float32)
    if shards:
        values = values * level_of(rng, shape, shards, -0.22, 0.18)
    return jnp.clip(values, -bound, bound).astype(kind)


def setup_inputs(seed: int = 0) -> dict:
    keys = jax.random.split(jax.random.key(seed), 7)
    return {
        "activity": gaussian(keys[0], (NC, NT), 1.0, 6.0, ((0, 32), (1, 4))),
        "drug_basis": draw_drug_basis(jax.random.fold_in(keys[6], 71), 0),
        "target_basis": draw_target_basis(jax.random.fold_in(keys[6], 71), 0),
        "drug_values": jnp.clip(jnp.exp(jax.random.uniform(keys[3], (R,), jnp.float32, math.log(0.05), math.log(20.0))), 0.05, 20.0),
        "target_values": jnp.clip(jnp.exp(jax.random.uniform(keys[4], (NT,), jnp.float32, math.log(0.05), math.log(20.0))), 0.05, 20.0),
        "ridge": jnp.clip(jnp.exp(jax.random.uniform(keys[5], (1,), jnp.float32, math.log(0.5), math.log(2.0))), 0.5, 2.0),
    }


def reference(activity, drug_basis, target_basis, drug_values, target_values, ridge):
    highest = lax.Precision.HIGHEST
    product = drug_values[:, None] * target_values[None, :]
    spectral_filter = product / (product + ridge[0])
    drug_sums = jnp.dot(drug_basis.T, activity, preferred_element_type=jnp.float32)
    target_wide = target_basis.astype(jnp.float32)
    coefficients = jnp.dot(drug_sums, target_wide, precision=highest, preferred_element_type=jnp.float32)
    filtered = spectral_filter * coefficients
    back_coeffs = jnp.dot(filtered, target_wide.T, precision=highest, preferred_element_type=jnp.float32)
    drug_wide = drug_basis.astype(jnp.float32)
    fitted_full = jnp.dot(drug_wide, back_coeffs, precision=highest, preferred_element_type=jnp.float32)
    target_squares = target_wide * target_wide
    lever_cols = jnp.dot(spectral_filter, target_squares.T, precision=highest, preferred_element_type=jnp.float32)
    drug_squares = drug_wide * drug_wide
    leverage = jnp.dot(drug_squares, lever_cols, precision=highest, preferred_element_type=jnp.float32)
    loo_residual = (activity.astype(jnp.float32) - fitted_full) / (1.0 - leverage)
    return fitted_full.astype(jnp.bfloat16), loo_residual.astype(jnp.bfloat16)
```

```python
import jax
import jax.numpy as jnp
from jax import lax
from jax.sharding import PartitionSpec as P


def halves(x):
    high = lax.reduce_precision(x, exponent_bits=8, mantissa_bits=7)
    return high.astype(jnp.bfloat16), (x - high).astype(jnp.bfloat16)


def dot(a, b, dims):
    return lax.dot_general(a, b, (dims, ((), ())), preferred_element_type=jnp.float32)


def shards(activity, drug_basis, target_basis, drug_values, target_values, ridge):
    drug_devices = lax.axis_size("cmp")
    target_devices = lax.axis_size("tgt")
    basis_rank = drug_basis.shape[1]
    target_local = target_basis.shape[0]
    drug_share = basis_rank // drug_devices
    drug_part = dot(drug_basis, activity, ((0,), (0,)))
    drug_parts = lax.all_to_all(
        drug_part.reshape(drug_devices, drug_share, target_local), "cmp", 0, 0
    )
    drug_block = drug_parts.sum(axis=0)
    high, low = halves(drug_block)
    coeff = dot(high, target_basis, ((1,), (0,))) + dot(low, target_basis, ((1,), (0,)))
    coeff = coeff + lax.ppermute(coeff, "tgt", [(i, i ^ 1) for i in range(target_devices)])
    coeff = coeff + lax.ppermute(coeff, "tgt", [(i, i ^ 2) for i in range(target_devices)])
    share_values = lax.dynamic_slice_in_dim(
        drug_values, lax.axis_index("cmp") * drug_share, drug_share
    )
    product = share_values[:, None] * target_values[None, :]
    filtered = product / (product + ridge[0]) * coeff
    high, low = halves(filtered)
    back = dot(high, target_basis, ((1,), (1,))) + dot(low, target_basis, ((1,), (1,)))
    back = lax.all_to_all(
        jnp.broadcast_to(back[None], (drug_devices, drug_share, target_local)), "cmp", 0, 0
    )
    high, low = halves(back.reshape(basis_rank, target_local))
    fitted_full = dot(drug_basis, high, ((1,), (0,))) + dot(drug_basis, low, ((1,), (0,)))
    target_wide = target_basis.astype(jnp.float32)
    square_high, square_low = halves(target_wide * target_wide)
    product = drug_values[:, None] * target_values[None, :]
    filter_high, filter_low = halves(product / (product + ridge[0]))
    lever_cols = (
        dot(filter_high, square_high, ((1,), (1,)))
        + dot(filter_high, square_low, ((1,), (1,)))
        + dot(filter_low, square_high, ((1,), (1,)))
    )
    lever_high, lever_low = halves(lever_cols)
    drug_wide = drug_basis.astype(jnp.float32)
    square_high, square_low = halves(drug_wide * drug_wide)
    leverage = (
        dot(square_high, lever_high, ((1,), (0,)))
        + dot(square_high, lever_low, ((1,), (0,)))
        + dot(square_low, lever_high, ((1,), (0,)))
    )
    loo_residual = (activity.astype(jnp.float32) - fitted_full) / (1.0 - leverage)
    return (fitted_full.astype(jnp.bfloat16), loo_residual.astype(jnp.bfloat16))


def solution(mesh):
    return jax.shard_map(
        shards,
        mesh=mesh,
        in_specs=(P("cmp", "tgt"), P("cmp", None), P("tgt", None), P(), P(), P()),
        out_specs=(P("cmp", "tgt"), P("cmp", "tgt")),
        check_vma=False,
    )
```

```python
import jax
import jax.numpy as jnp
from jax import lax
from jax.experimental import pallas as pl
from jax.experimental.pallas import tpu as pltpu
from jax.sharding import PartitionSpec as P

MIB = 1024 * 1024


def halves(x):
    high = x.astype(jnp.bfloat16)
    return high, (x - high.astype(jnp.float32)).astype(jnp.bfloat16)


def dot(a, b, dims):
    return lax.dot_general(a, b, (dims, ((), ())), preferred_element_type=jnp.float32)


def dot_halves(x, b, dims):
    rows = x.shape[0]
    out = dot(jnp.concatenate(halves(x), axis=0), b, dims)
    return out[:rows] + out[rows:]


def crossed():
    return lax.axis_index("tgt") // 2


def project(drug_basis, activity, out):
    devices, share, _ = out.shape
    sums = dot(drug_basis[...], activity[...], ((0,), (0,)))
    flip = crossed()
    for k in range(devices):
        out[jnp.int32(k) ^ flip] = sums[k * share : (k + 1) * share]


def lever(drug_values, target_values, ridge, target_basis, drug_basis, inverse, weights):
    rank, share = drug_values.shape[1], weights.shape[0]
    values, columns, offset = drug_values[...], target_values[...], ridge[0]

    def spectral(first, rows):
        lane = lax.broadcasted_iota(jnp.int32, (rows, rank), 1)
        row = lax.broadcasted_iota(jnp.int32, (rows, rank), 0)
        own = jnp.where(lane == row + first, values, 0.0).sum(axis=1, keepdims=True)
        product = own * columns
        return product / (product + offset)

    weights[...] = spectral((lax.axis_index("cmp") ^ crossed()) * share, share)
    filter_high, filter_low = halves(spectral(0, rank))
    wide = target_basis[...].astype(jnp.float32)
    square_high, square_low = halves(wide * wide)
    along = ((1,), (1,))
    cols = (
        dot(filter_high, square_high, along)
        + dot(filter_high, square_low, along)
        + dot(filter_low, square_high, along)
    )
    cols_high, cols_low = halves(cols)
    wide = drug_basis[...].astype(jnp.float32)
    square_high, square_low = halves(wide * wide)
    along = ((1,), (0,))
    leverage = (
        dot(square_high, cols_high, along)
        + dot(square_high, cols_low, along)
        + dot(square_low, cols_high, along)
    )
    inverse[...] = 1.0 / (1.0 - leverage)


def forward(parts, target_basis, weights, out):
    out[...] = weights[...] * dot_halves(parts[...].sum(axis=0), target_basis[...], ((1,), (0,)))


def backward(mine, other, target_basis, out):
    back = dot_halves(mine[...] + other[...], target_basis[...], ((1,), (1,)))
    out[...] = jnp.broadcast_to(back[None], out.shape)


def fit(parts, drug_basis, activity, inverse, fitted, residual, high, low):
    devices, share, _ = parts.shape
    flip = crossed()
    for k in range(devices):
        rows = pl.ds(k * share, share)
        high[rows], low[rows] = halves(parts[jnp.int32(k) ^ flip])
    basis = drug_basis[...]
    full = dot(basis, high[...], ((1,), (0,))) + dot(basis, low[...], ((1,), (0,)))
    fitted[...] = full.astype(fitted.dtype)
    wide = activity[...].astype(jnp.float32)
    residual[...] = ((wide - full) * inverse[...]).astype(residual.dtype)


def call(body, outs, flops, scratch=(), smem=()):
    def run(*args):
        vmem = pl.BlockSpec(memory_space=pltpu.VMEM)
        scalar = pl.BlockSpec(memory_space=pltpu.SMEM)
        return pl.pallas_call(
            body,
            out_shape=outs,
            in_specs=[scalar if i in smem else vmem for i in range(len(args))],
            out_specs=jax.tree.map(lambda _: vmem, outs),
            scratch_shapes=list(scratch),
            compiler_params=pltpu.CompilerParams(vmem_limit_bytes=40 * MIB),
            cost_estimate=pl.CostEstimate(
                flops=flops, bytes_accessed=sum(x.size * x.dtype.itemsize for x in args), transcendentals=0
            ),
            name=body.__name__,
        )(*args)

    return run


def shards(activity, drug_basis, target_basis, drug_values, target_values, ridge):
    drug_devices = lax.axis_size("cmp")
    target_devices = lax.axis_size("tgt")
    compounds, rank = drug_basis.shape
    targets_here, targets = target_basis.shape
    share = rank // drug_devices
    devices = range(drug_devices * target_devices)
    f32, bf16 = jnp.float32, jnp.bfloat16
    blocks = jax.ShapeDtypeStruct((drug_devices, share, targets_here), f32)
    rows = jax.ShapeDtypeStruct((share, targets), f32)
    here = jax.ShapeDtypeStruct((compounds, targets_here), f32)
    output = jax.ShapeDtypeStruct((compounds, targets_here), bf16)

    sums = call(project, blocks, 2 * compounds * rank * targets_here)(drug_basis, activity)
    parts = lax.all_to_all(sums, "cmp", 0, 0)
    inverse, weights = call(
        lever, (here, rows), 6 * rank * targets_here * (targets + compounds), smem=(2,)
    )(drug_values[None], target_values[None], ridge, target_basis, drug_basis)
    coeff = call(forward, rows, 4 * share * targets_here * targets)(parts, target_basis, weights)
    coeff = coeff + lax.ppermute(coeff, "tgt", [(i, i ^ 1) for i in range(target_devices)])
    across = target_devices | 2
    other = lax.ppermute(coeff, ("cmp", "tgt"), [(i, i ^ across) for i in devices])
    back = call(backward, blocks, 4 * share * targets_here * targets)(coeff, other, target_basis)
    back = lax.all_to_all(back, "cmp", 0, 0)
    scratch = (pltpu.VMEM((rank, targets_here), bf16),) * 2
    return call(fit, (output, output), 4 * compounds * rank * targets_here, scratch)(
        back, drug_basis, activity, inverse
    )


def solution(mesh):
    return jax.shard_map(
        shards,
        mesh=mesh,
        in_specs=(P("cmp", "tgt"), P("cmp", None), P("tgt", None), P(), P(), P()),
        out_specs=(P("cmp", "tgt"), P("cmp", "tgt")),
        check_vma=False,
    )
```

```python
import jax
import jax.numpy as jnp
from jax import lax
from jax.experimental import pallas as pl
from jax.experimental.pallas import tpu as pltpu
from jax.sharding import PartitionSpec as P

MIB = 1024 * 1024


def halves(x):
    high = x.astype(jnp.bfloat16)
    return high, (x - high.astype(jnp.float32)).astype(jnp.bfloat16)


def dot(a, b, dims):
    return lax.dot_general(a, b, (dims, ((), ())), preferred_element_type=jnp.float32)


def dot_halves(x, b, dims):
    rows = x.shape[0]
    out = dot(jnp.concatenate(halves(x), axis=0), b, dims)
    return out[:rows] + out[rows:]


def crossed():
    return lax.axis_index("tgt") // 2


def project(drug_basis, activity, out, basis, values, sems):
    devices, share, _ = out.shape
    copies = [
        pltpu.make_async_copy(drug_basis, basis, sems.at[0]),
        pltpu.make_async_copy(activity, values, sems.at[1]),
    ]
    for copy in copies:
        copy.start()
    for copy in copies:
        copy.wait()
    sums = dot(basis[...], values[...], ((0,), (0,)))
    flip = crossed()
    for k in range(devices):
        out[jnp.int32(k) ^ flip] = sums[k * share : (k + 1) * share]


def lever(drug_values, target_values, ridge, target_basis, drug_basis, _, inverse, weights):
    rank, share = drug_values.shape[1], weights.shape[0]
    values, columns, offset = drug_values[...], target_values[...], ridge[0]

    def spectral(first, rows):
        lane = lax.broadcasted_iota(jnp.int32, (rows, rank), 1)
        row = lax.broadcasted_iota(jnp.int32, (rows, rank), 0)
        own = jnp.where(lane == row + first, values, 0.0).sum(axis=1, keepdims=True)
        product = own * columns
        return product / (product + offset)

    weights[...] = spectral((lax.axis_index("cmp") ^ crossed()) * share, share)
    filter_high, filter_low = halves(spectral(0, rank))
    wide = target_basis[...].astype(jnp.float32)
    square_high, square_low = halves(wide * wide)
    along = ((1,), (1,))
    cols = (
        dot(filter_high, square_high, along)
        + dot(filter_high, square_low, along)
        + dot(filter_low, square_high, along)
    )
    cols_high, cols_low = halves(cols)
    wide = drug_basis[...].astype(jnp.float32)
    square_high, square_low = halves(wide * wide)
    along = ((1,), (0,))
    leverage = (
        dot(square_high, cols_high, along)
        + dot(square_high, cols_low, along)
        + dot(square_low, cols_high, along)
    )
    inverse[...] = 1.0 / (1.0 - leverage)


def forward(parts, target_basis, out):
    out[...] = dot_halves(parts[...].sum(axis=0), target_basis[...], ((1,), (0,)))


def backward(mine, other, weights, target_basis, out):
    back = dot_halves(weights[...] * (mine[...] + other[...]), target_basis[...], ((1,), (1,)))
    out[...] = jnp.broadcast_to(back[None], out.shape)


def fit(parts, drug_basis, activity, inverse, fitted, residual, high, low):
    devices, share, _ = parts.shape
    flip = crossed()
    for k in range(devices):
        rows = pl.ds(k * share, share)
        high[rows], low[rows] = halves(parts[jnp.int32(k) ^ flip])
    basis = drug_basis[...]
    full = dot(basis, high[...], ((1,), (0,))) + dot(basis, low[...], ((1,), (0,)))
    fitted[...] = full.astype(fitted.dtype)
    wide = activity[...].astype(jnp.float32)
    residual[...] = ((wide - full) * inverse[...]).astype(residual.dtype)


def call(body, outs, flops, scratch=(), smem=(), hbm=(), hbm_out=False):
    def run(*args):
        vmem = pl.BlockSpec(memory_space=pltpu.VMEM)
        scalar = pl.BlockSpec(memory_space=pltpu.SMEM)
        far = pl.BlockSpec(memory_space=pltpu.HBM)
        return pl.pallas_call(
            body,
            out_shape=outs,
            in_specs=[scalar if i in smem else far if i in hbm else vmem for i in range(len(args))],
            out_specs=jax.tree.map(lambda _: far if hbm_out else vmem, outs),
            scratch_shapes=list(scratch),
            compiler_params=pltpu.CompilerParams(vmem_limit_bytes=40 * MIB),
            cost_estimate=pl.CostEstimate(
                flops=flops, bytes_accessed=sum(x.size * x.dtype.itemsize for x in args), transcendentals=0
            ),
            name=body.__name__,
        )(*args)

    return run


def shards(activity, drug_basis, target_basis, drug_values, target_values, ridge):
    drug_devices = lax.axis_size("cmp")
    target_devices = lax.axis_size("tgt")
    compounds, rank = drug_basis.shape
    targets_here, targets = target_basis.shape
    share = rank // drug_devices
    devices = range(drug_devices * target_devices)
    f32, bf16 = jnp.float32, jnp.bfloat16
    blocks = jax.ShapeDtypeStruct((drug_devices, share, targets_here), f32)
    rows = jax.ShapeDtypeStruct((share, targets), f32)
    here = jax.ShapeDtypeStruct((compounds, targets_here), f32)
    output = jax.ShapeDtypeStruct((compounds, targets_here), bf16)

    scratch = (
        pltpu.VMEM(drug_basis.shape, bf16),
        pltpu.VMEM(activity.shape, bf16),
        pltpu.SemaphoreType.DMA((2,)),
    )
    far = [pltpu.with_memory_space_constraint(x, pltpu.HBM) for x in (drug_basis, activity)]
    sums = call(project, blocks, 2 * compounds * rank * targets_here, scratch, hbm=(0, 1))(*far)
    parts = lax.all_to_all(sums, "cmp", 0, 0)
    coeff = call(forward, rows, 4 * share * targets_here * targets)(parts, target_basis)
    coeff = coeff + lax.ppermute(coeff, "tgt", [(i, i ^ 1) for i in range(target_devices)])
    across = target_devices | 2
    inverse, weights = call(
        lever, (here, rows), 6 * rank * targets_here * (targets + compounds), smem=(2,), hbm=(5,)
    )(drug_values[None], target_values[None], ridge, target_basis, drug_basis, coeff)
    other = lax.ppermute(coeff, ("cmp", "tgt"), [(i, i ^ across) for i in devices])
    back = call(backward, blocks, 4 * share * targets_here * targets)(coeff, other, weights, target_basis)
    back = lax.all_to_all(back, "cmp", 0, 0)
    scratch = (pltpu.VMEM((rank, targets_here), bf16),) * 2
    return call(fit, (output, output), 4 * compounds * rank * targets_here, scratch)(
        back, drug_basis, activity, inverse
    )


def solution(mesh):
    return jax.shard_map(
        shards,
        mesh=mesh,
        in_specs=(P("cmp", "tgt"), P("cmp", None), P("tgt", None), P(), P(), P()),
        out_specs=(P("cmp", "tgt"), P("cmp", "tgt")),
        check_vma=False,
    )
```

```python
import jax
import jax.numpy as jnp
from jax import lax
from jax.experimental import pallas as pl
from jax.experimental.pallas import tpu as pltpu
from jax.sharding import PartitionSpec as P

MIB = 1024 * 1024
PIECES = 2


def halves(x):
    high = x.astype(jnp.bfloat16)
    return high, (x - high.astype(jnp.float32)).astype(jnp.bfloat16)


def dot(a, b, along=(1, 0)):
    dims = (((along[0],), (along[1],)), ((), ()))
    return lax.dot_general(a, b, dims, preferred_element_type=jnp.float32)


def dot_halves(x, b):
    rows = x.shape[0]
    out = dot(jnp.concatenate(halves(x), axis=0), b)
    return out[:rows] + out[rows:]


def dot_pairs(a, b):
    rows = a[0].shape[0]
    out = dot(jnp.concatenate(a, axis=0), b[0])
    return out[:rows] + out[rows:] + dot(a[0], b[1])


def core():
    return lax.rem(lax.axis_index("tgt"), 2)


def crossed():
    return lax.axis_index("tgt") // 2


def eigen(drug_values, first, rows):
    rank = drug_values.shape[1]
    lane = lax.broadcasted_iota(jnp.int32, (rows, rank), 1)
    row = lax.broadcasted_iota(jnp.int32, (rows, rank), 0)
    return jnp.where(lane == row + first, drug_values[...], 0.0).sum(axis=1, keepdims=True)


def project(drug_basis, activity, out, basis, values, sems):
    devices, share, _ = out.shape
    copies = [
        pltpu.make_async_copy(drug_basis, basis, sems.at[0]),
        pltpu.make_async_copy(activity, values, sems.at[1]),
    ]
    for copy in copies:
        copy.start()
    for copy in copies:
        copy.wait()
    sums = dot(basis[...], values[...], (0, 0))
    flip = crossed()
    for k in range(devices):
        out[jnp.int32(k) ^ flip] = sums[k * share : (k + 1) * share]


def forward(parts, target_basis, out, turned):
    out[...] = dot_halves(parts[...].sum(axis=0), target_basis[...])

    @pl.when(core() == 1)
    def _():
        turned[...] = target_basis[...].T


def middle(mine, other, target_basis, out, turned):
    out[...] = mine[...] + other[...]

    @pl.when(core() == 0)
    def _():
        turned[...] = target_basis[...].T


def of_core(work, turned_0, turned_1):
    @pl.when(core() == 0)
    def _():
        work(turned_0)

    @pl.when(core() == 1)
    def _():
        work(turned_1)


def lever(drug_values, target_values, ridge, drug_basis, turned_0, turned_1, inverse, weights):
    rank, targets, share = drug_values.shape[1], target_values.shape[1], weights.shape[0]
    offset = ridge[0]
    first = (lax.axis_index("cmp") ^ crossed()) * share
    product = eigen(drug_values, first, share) * target_values[...]
    weights[...] = product / (product + offset)
    wide = drug_basis[...].astype(jnp.float32)
    squares = halves(wide * wide)
    own = eigen(drug_values, 0, rank)

    def work(turned):
        step = targets // PIECES
        total = None
        for start in range(0, targets, step):
            some = slice(start, start + step)
            product = own * target_values[:, some]
            mixed = dot_pairs(squares, halves(product / (product + offset)))
            wide = turned[some].astype(jnp.float32)
            term = dot_pairs(halves(mixed), halves(wide * wide))
            total = term if total is None else total + term
        inverse[...] = 1.0 / (1.0 - total)

    of_core(work, turned_0, turned_1)


def backward(mine, other, weights, turned_0, turned_1, out):
    filtered = weights[...] * (mine[...] + other[...])

    def work(turned):
        out[...] = jnp.broadcast_to(dot_halves(filtered, turned[...])[None], out.shape)

    of_core(work, turned_0, turned_1)


def fit(parts, drug_basis, activity, inverse, fitted, residual, high, low):
    devices, share, _ = parts.shape
    flip = crossed()
    for k in range(devices):
        rows = pl.ds(k * share, share)
        high[rows], low[rows] = halves(parts[jnp.int32(k) ^ flip])
    basis = drug_basis[...]
    full = dot(basis, high[...]) + dot(basis, low[...])
    fitted[...] = full.astype(fitted.dtype)
    wide = activity[...].astype(jnp.float32)
    residual[...] = ((wide - full) * inverse[...]).astype(residual.dtype)


def call(body, outs, flops, scratch=(), far=(), scalar=()):
    def run(*args):
        vmem = pl.BlockSpec(memory_space=pltpu.VMEM)
        spaces = {**dict.fromkeys(far, pl.ANY), **dict.fromkeys(scalar, pltpu.SMEM)}
        return pl.pallas_call(
            body,
            out_shape=outs,
            in_specs=[pl.BlockSpec(memory_space=spaces.get(i, pltpu.VMEM)) for i in range(len(args))],
            out_specs=jax.tree.map(lambda _: vmem, outs),
            scratch_shapes=list(scratch),
            compiler_params=pltpu.CompilerParams(vmem_limit_bytes=40 * MIB),
            cost_estimate=pl.CostEstimate(
                flops=flops, bytes_accessed=sum(x.size * x.dtype.itemsize for x in args), transcendentals=0
            ),
            name=body.__name__,
        )(*args)

    return run


def shards(activity, drug_basis, target_basis, drug_values, target_values, ridge):
    drug_devices = lax.axis_size("cmp")
    target_devices = lax.axis_size("tgt")
    compounds, rank = drug_basis.shape
    targets_here, targets = target_basis.shape
    share = rank // drug_devices
    devices = range(drug_devices * target_devices)
    f32, bf16 = jnp.float32, jnp.bfloat16
    blocks = jax.ShapeDtypeStruct((drug_devices, share, targets_here), f32)
    rows = jax.ShapeDtypeStruct((share, targets), f32)
    here = jax.ShapeDtypeStruct((compounds, targets_here), f32)
    turned = jax.ShapeDtypeStruct((targets, targets_here), bf16)
    output = jax.ShapeDtypeStruct((compounds, targets_here), bf16)

    scratch = (
        pltpu.VMEM(drug_basis.shape, bf16),
        pltpu.VMEM(activity.shape, bf16),
        pltpu.SemaphoreType.DMA((2,)),
    )
    far = [pltpu.with_memory_space_constraint(x, pltpu.HBM) for x in (drug_basis, activity)]
    sums = call(project, blocks, 2 * compounds * rank * targets_here, scratch, far=(0, 1))(*far)
    parts = lax.all_to_all(sums, "cmp", 0, 0)
    flops = 4 * share * targets_here * targets
    coeff, turned_1 = call(forward, (rows, turned), flops)(parts, target_basis)
    other = lax.ppermute(coeff, "tgt", [(i, i ^ 1) for i in range(target_devices)])
    coeff, turned_0 = call(middle, (rows, turned), targets_here * targets)(coeff, other, target_basis)
    across = target_devices | 2
    other = lax.ppermute(coeff, ("cmp", "tgt"), [(i, i ^ across) for i in devices])
    inverse, weights = call(lever, (here, rows), 6 * compounds * rank * targets, scalar=(2,))(
        drug_values[None], target_values[None], ridge, drug_basis, turned_0, turned_1
    )
    back = call(backward, blocks, flops)(coeff, other, weights, turned_0, turned_1)
    back = lax.all_to_all(back, "cmp", 0, 0)
    scratch = (pltpu.VMEM((rank, targets_here), bf16),) * 2
    return call(fit, (output, output), 4 * compounds * rank * targets_here, scratch)(
        back, drug_basis, activity, inverse
    )


def solution(mesh):
    return jax.shard_map(
        shards,
        mesh=mesh,
        in_specs=(P("cmp", "tgt"), P("cmp", None), P("tgt", None), P(), P(), P()),
        out_specs=(P("cmp", "tgt"), P("cmp", "tgt")),
        check_vma=False,
    )
```

```python
import jax
import jax.numpy as jnp
from jax import lax
from jax.experimental import pallas as pl
from jax.experimental.pallas import tpu as pltpu
from jax.sharding import PartitionSpec as P

MIB = 1024 * 1024
PIECES = 2


def halves(x):
    high = x.astype(jnp.bfloat16)
    return high, (x - high.astype(jnp.float32)).astype(jnp.bfloat16)


def dot(a, b, along=(1, 0)):
    dims = (((along[0],), (along[1],)), ((), ()))
    return lax.dot_general(a, b, dims, preferred_element_type=jnp.float32)


def dot_halves(x, b):
    rows = x.shape[0]
    out = dot(jnp.concatenate(halves(x), axis=0), b)
    return out[:rows] + out[rows:]


def dot_pairs(a, b):
    rows = a[0].shape[0]
    out = dot(jnp.concatenate(a, axis=0), b[0])
    return out[:rows] + out[rows:] + dot(a[0], b[1])


def core():
    return lax.rem(lax.axis_index("tgt"), 2)


def owners(drug_devices, target_devices):
    here = range(drug_devices // 2)
    return [
        [(2 * place + (low ^ block // 2)) * target_devices + block for low in range(2) for place in here]
        for block in range(target_devices)
    ]


def owned():
    place, block = lax.axis_index("cmp"), lax.axis_index("tgt")
    return (lax.rem(place, 2) ^ (block // 2)) * (lax.axis_size("cmp") // 2) + place // 2


def eigen(drug_values, first, rows):
    rank = drug_values.shape[1]
    lane = lax.broadcasted_iota(jnp.int32, (rows, rank), 1)
    row = lax.broadcasted_iota(jnp.int32, (rows, rank), 0)
    return jnp.where(lane == row + first, drug_values[...], 0.0).sum(axis=1, keepdims=True)


def project(drug_basis, activity, out, basis, values, sems):
    devices, share, width = out.shape
    copies = [
        pltpu.make_async_copy(drug_basis, basis, sems.at[0]),
        pltpu.make_async_copy(activity, values, sems.at[1]),
    ]
    for copy in copies:
        copy.start()
    for copy in copies:
        copy.wait()
    sums = dot(basis[...], values[...], (0, 0))
    out[...] = sums.reshape(devices, share, width)


def forward(parts, target_basis, out, turned):
    out[...] = dot_halves(parts[...].sum(axis=0), target_basis[...])

    @pl.when(core() == 1)
    def _():
        turned[...] = target_basis[...].T


def middle(mine, other, target_basis, out, turned):
    out[...] = mine[...] + other[...]

    @pl.when(core() == 0)
    def _():
        turned[...] = target_basis[...].T


def of_core(work, turned_0, turned_1):
    @pl.when(core() == 0)
    def _():
        work(turned_0)

    @pl.when(core() == 1)
    def _():
        work(turned_1)


def lever(drug_values, target_values, ridge, drug_basis, turned_0, turned_1, inverse, weights):
    rank, targets, share = drug_values.shape[1], target_values.shape[1], weights.shape[0]
    offset = ridge[0]
    product = eigen(drug_values, owned() * share, share) * target_values[...]
    weights[...] = product / (product + offset)
    wide = drug_basis[...].astype(jnp.float32)
    squares = halves(wide * wide)
    own = eigen(drug_values, 0, rank)

    def work(turned):
        step = targets // PIECES
        total = None
        for start in range(0, targets, step):
            some = slice(start, start + step)
            product = own * target_values[:, some]
            mixed = dot_pairs(squares, halves(product / (product + offset)))
            wide = turned[some].astype(jnp.float32)
            term = dot_pairs(halves(mixed), halves(wide * wide))
            total = term if total is None else total + term
        inverse[...] = 1.0 / (1.0 - total)

    of_core(work, turned_0, turned_1)


def backward(mine, other, weights, turned_0, turned_1, out):
    filtered = weights[...] * (mine[...] + other[...])

    def work(turned):
        out[...] = jnp.broadcast_to(dot_halves(filtered, turned[...])[None], out.shape)

    of_core(work, turned_0, turned_1)


def fit(parts, drug_basis, activity, inverse, fitted, residual):
    devices, share, width = parts.shape
    high, low = halves(parts[...].reshape(devices * share, width))
    basis = drug_basis[...]
    full = dot(basis, high) + dot(basis, low)
    fitted[...] = full.astype(fitted.dtype)
    wide = activity[...].astype(jnp.float32)
    residual[...] = ((wide - full) * inverse[...]).astype(residual.dtype)


def call(body, outs, flops, scratch=(), far=(), scalar=()):
    def run(*args):
        vmem = pl.BlockSpec(memory_space=pltpu.VMEM)
        spaces = {**dict.fromkeys(far, pl.ANY), **dict.fromkeys(scalar, pltpu.SMEM)}
        return pl.pallas_call(
            body,
            out_shape=outs,
            in_specs=[pl.BlockSpec(memory_space=spaces.get(i, pltpu.VMEM)) for i in range(len(args))],
            out_specs=jax.tree.map(lambda _: vmem, outs),
            scratch_shapes=list(scratch),
            compiler_params=pltpu.CompilerParams(vmem_limit_bytes=40 * MIB),
            cost_estimate=pl.CostEstimate(
                flops=flops, bytes_accessed=sum(x.size * x.dtype.itemsize for x in args), transcendentals=0
            ),
            name=body.__name__,
        )(*args)

    return run


def shards(activity, drug_basis, target_basis, drug_values, target_values, ridge):
    drug_devices = lax.axis_size("cmp")
    target_devices = lax.axis_size("tgt")
    compounds, rank = drug_basis.shape
    targets_here, targets = target_basis.shape
    share = rank // drug_devices
    devices = range(drug_devices * target_devices)
    f32, bf16 = jnp.float32, jnp.bfloat16
    blocks = jax.ShapeDtypeStruct((drug_devices, share, targets_here), f32)
    rows = jax.ShapeDtypeStruct((share, targets), f32)
    here = jax.ShapeDtypeStruct((compounds, targets_here), f32)
    turned = jax.ShapeDtypeStruct((targets, targets_here), bf16)
    output = jax.ShapeDtypeStruct((compounds, targets_here), bf16)

    scratch = (
        pltpu.VMEM(drug_basis.shape, bf16),
        pltpu.VMEM(activity.shape, bf16),
        pltpu.SemaphoreType.DMA((2,)),
    )
    far = [pltpu.with_memory_space_constraint(x, pltpu.HBM) for x in (drug_basis, activity)]
    sums = call(project, blocks, 2 * compounds * rank * targets_here, scratch, far=(0, 1))(*far)
    groups = owners(drug_devices, target_devices)
    parts = lax.all_to_all(sums, ("cmp", "tgt"), 0, 0, axis_index_groups=groups)
    flops = 4 * share * targets_here * targets
    coeff, turned_1 = call(forward, (rows, turned), flops)(parts, target_basis)
    other = lax.ppermute(coeff, "tgt", [(i, i ^ 1) for i in range(target_devices)])
    coeff, turned_0 = call(middle, (rows, turned), targets_here * targets)(coeff, other, target_basis)
    across = target_devices | 2
    other = lax.ppermute(coeff, ("cmp", "tgt"), [(i, i ^ across) for i in devices])
    inverse, weights = call(lever, (here, rows), 6 * compounds * rank * targets, scalar=(2,))(
        drug_values[None], target_values[None], ridge, drug_basis, turned_0, turned_1
    )
    back = call(backward, blocks, flops)(coeff, other, weights, turned_0, turned_1)
    back = lax.all_to_all(back, ("cmp", "tgt"), 0, 0, axis_index_groups=groups)
    return call(fit, (output, output), 4 * compounds * rank * targets_here)(
        back, drug_basis, activity, inverse
    )


def solution(mesh):
    return jax.shard_map(
        shards,
        mesh=mesh,
        in_specs=(P("cmp", "tgt"), P("cmp", None), P("tgt", None), P(), P(), P()),
        out_specs=(P("cmp", "tgt"), P("cmp", "tgt")),
        check_vma=False,
    )
```

```python
import jax
import jax.numpy as jnp
from jax import lax
from jax.experimental import pallas as pl
from jax.experimental.pallas import tpu as pltpu
from jax.sharding import PartitionSpec as P

MIB = 1024 * 1024
PIECES, LATE = 4, 1


def halves(x):
    high = x.astype(jnp.bfloat16)
    return high, (x - high.astype(jnp.float32)).astype(jnp.bfloat16)


def dot(a, b, along=(1, 0)):
    dims = (((along[0],), (along[1],)), ((), ()))
    return lax.dot_general(a, b, dims, preferred_element_type=jnp.float32)


def dot_halves(x, b):
    rows = x.shape[0]
    out = dot(jnp.concatenate(halves(x), axis=0), b)
    return out[:rows] + out[rows:]


def dot_pairs(a, b):
    rows = a[0].shape[0]
    out = dot(jnp.concatenate(a, axis=0), b[0])
    return out[:rows] + out[rows:] + dot(a[0], b[1])


def core():
    return lax.rem(lax.axis_index("tgt"), 2)


def owners(drug_devices, target_devices):
    here = range(drug_devices // 2)
    return [
        [(2 * place + (low ^ block // 2)) * target_devices + block for low in range(2) for place in here]
        for block in range(target_devices)
    ]


def owned():
    place, block = lax.axis_index("cmp"), lax.axis_index("tgt")
    return (lax.rem(place, 2) ^ (block // 2)) * (lax.axis_size("cmp") // 2) + place // 2


def eigen(drug_values, first, rows):
    rank = drug_values.shape[1]
    lane = lax.broadcasted_iota(jnp.int32, (rows, rank), 1)
    row = lax.broadcasted_iota(jnp.int32, (rows, rank), 0)
    return jnp.where(lane == row + first, drug_values[...], 0.0).sum(axis=1, keepdims=True)


def project(drug_basis, activity, out, basis, values, sems):
    devices, share, width = out.shape
    copies = [
        pltpu.make_async_copy(drug_basis, basis, sems.at[0]),
        pltpu.make_async_copy(activity, values, sems.at[1]),
    ]
    for copy in copies:
        copy.start()
    for copy in copies:
        copy.wait()
    sums = dot(basis[...], values[...], (0, 0))
    out[...] = sums.reshape(devices, share, width)


def forward(parts, target_basis, out, turned):
    out[...] = dot_halves(parts[...].sum(axis=0), target_basis[...])

    @pl.when(core() == 1)
    def _():
        turned[...] = target_basis[...].T


def middle(mine, other, target_basis, out, turned):
    out[...] = mine[...] + other[...]

    @pl.when(core() == 0)
    def _():
        turned[...] = target_basis[...].T


def of_core(work, turned_0, turned_1):
    @pl.when(core() == 0)
    def _():
        work(turned_0)

    @pl.when(core() == 1)
    def _():
        work(turned_1)


def leverage(drug_values, target_values, ridge, drug_basis, turned, pieces):
    wide = drug_basis[...].astype(jnp.float32)
    squares = halves(wide * wide)
    own = eigen(drug_values, 0, drug_values.shape[1])
    step = target_values.shape[1] // PIECES
    total = None
    for piece in pieces:
        some = slice(piece * step, (piece + 1) * step)
        product = own * target_values[:, some]
        mixed = dot_pairs(squares, halves(product / (product + ridge[0])))
        wide = turned[some].astype(jnp.float32)
        term = dot_pairs(halves(mixed), halves(wide * wide))
        total = term if total is None else total + term
    return total


def lever(drug_values, target_values, ridge, drug_basis, turned_0, turned_1, total, weights):
    values = drug_values, target_values, ridge, drug_basis
    product = eigen(drug_values, owned() * weights.shape[0], weights.shape[0]) * target_values[...]
    weights[...] = product / (product + ridge[0])

    @pl.when(core() == 0)
    def _():
        total[...] = leverage(*values, turned_0, range(PIECES))

    @pl.when(core() == 1)
    def _():
        total[...] = leverage(*values, turned_1, range(PIECES - LATE))


def backward(mine, other, weights, turned_0, turned_1, out):
    filtered = weights[...] * (mine[...] + other[...])

    def work(turned):
        out[...] = jnp.broadcast_to(dot_halves(filtered, turned[...])[None], out.shape)

    of_core(work, turned_0, turned_1)


def fit(parts, activity, total, drug_values, target_values, ridge, drug_basis, turned_1, fitted, residual, rest):
    devices, share, width = parts.shape
    rest[...] = total[...]

    @pl.when(core() == 1)
    def _():
        late = range(PIECES - LATE, PIECES)
        rest[...] += leverage(drug_values, target_values, ridge, drug_basis, turned_1, late)

    high, low = halves(parts[...].reshape(devices * share, width))
    basis = drug_basis[...]
    full = dot(basis, high) + dot(basis, low)
    fitted[...] = full.astype(fitted.dtype)
    wide = activity[...].astype(jnp.float32)
    residual[...] = ((wide - full) / (1.0 - rest[...])).astype(residual.dtype)


def call(body, outs, flops, scratch=(), far=(), scalar=()):
    def run(*args):
        vmem = pl.BlockSpec(memory_space=pltpu.VMEM)
        spaces = {**dict.fromkeys(far, pl.ANY), **dict.fromkeys(scalar, pltpu.SMEM)}
        return pl.pallas_call(
            body,
            out_shape=outs,
            in_specs=[pl.BlockSpec(memory_space=spaces.get(i, pltpu.VMEM)) for i in range(len(args))],
            out_specs=jax.tree.map(lambda _: vmem, outs),
            scratch_shapes=list(scratch),
            compiler_params=pltpu.CompilerParams(vmem_limit_bytes=40 * MIB),
            cost_estimate=pl.CostEstimate(
                flops=flops, bytes_accessed=sum(x.size * x.dtype.itemsize for x in args), transcendentals=0
            ),
            name=body.__name__,
        )(*args)

    return run


def shards(activity, drug_basis, target_basis, drug_values, target_values, ridge):
    drug_devices = lax.axis_size("cmp")
    target_devices = lax.axis_size("tgt")
    compounds, rank = drug_basis.shape
    targets_here, targets = target_basis.shape
    share = rank // drug_devices
    devices = range(drug_devices * target_devices)
    f32, bf16 = jnp.float32, jnp.bfloat16
    blocks = jax.ShapeDtypeStruct((drug_devices, share, targets_here), f32)
    rows = jax.ShapeDtypeStruct((share, targets), f32)
    here = jax.ShapeDtypeStruct((compounds, targets_here), f32)
    turned = jax.ShapeDtypeStruct((targets, targets_here), bf16)
    output = jax.ShapeDtypeStruct((compounds, targets_here), bf16)

    scratch = (
        pltpu.VMEM(drug_basis.shape, bf16),
        pltpu.VMEM(activity.shape, bf16),
        pltpu.SemaphoreType.DMA((2,)),
    )
    far = [pltpu.with_memory_space_constraint(x, pltpu.HBM) for x in (drug_basis, activity)]
    sums = call(project, blocks, 2 * compounds * rank * targets_here, scratch, far=(0, 1))(*far)
    groups = owners(drug_devices, target_devices)
    parts = lax.all_to_all(sums, ("cmp", "tgt"), 0, 0, axis_index_groups=groups)
    flops = 4 * share * targets_here * targets
    coeff, turned_1 = call(forward, (rows, turned), flops)(parts, target_basis)
    other = lax.ppermute(coeff, "tgt", [(i, i ^ 1) for i in range(target_devices)])
    coeff, turned_0 = call(middle, (rows, turned), targets_here * targets)(coeff, other, target_basis)
    across = target_devices | 2
    other = lax.ppermute(coeff, ("cmp", "tgt"), [(i, i ^ across) for i in devices])
    values = (drug_values[None], target_values[None], ridge, drug_basis)
    total, weights = call(lever, (here, rows), 6 * compounds * rank * targets, scalar=(2,))(
        *values, turned_0, turned_1
    )
    back = call(backward, blocks, flops)(coeff, other, weights, turned_0, turned_1)
    back = lax.all_to_all(back, ("cmp", "tgt"), 0, 0, axis_index_groups=groups)
    scratch = (pltpu.VMEM(here.shape, f32),)
    return call(fit, (output, output), 4 * compounds * rank * targets_here, scratch, scalar=(5,))(
        back, activity, total, *values, turned_1
    )


def solution(mesh):
    return jax.shard_map(
        shards,
        mesh=mesh,
        in_specs=(P("cmp", "tgt"), P("cmp", None), P("tgt", None), P(), P(), P()),
        out_specs=(P("cmp", "tgt"), P("cmp", "tgt")),
        check_vma=False,
    )
```

```python
import jax
import jax.numpy as jnp
from jax import lax
from jax.experimental import pallas as pl
from jax.experimental.pallas import tpu as pltpu
from jax.sharding import PartitionSpec as P

MIB = 1024 * 1024
PLANE, Z = 16, 4
AHEAD = (2, 1)
PIECES, LATE = 4, 1


def halves(x):
    high = x.astype(jnp.bfloat16)
    return high, (x - high.astype(jnp.float32)).astype(jnp.bfloat16)


def dot(a, b, along=(1, 0)):
    dims = (((along[0],), (along[1],)), ((), ()))
    return lax.dot_general(a, b, dims, preferred_element_type=jnp.float32)


def dot_halves(x, b):
    rows = x.shape[0]
    out = dot(jnp.concatenate(halves(x), axis=0), b)
    return out[:rows] + out[rows:]


def dot_pairs(a, b):
    rows = a[0].shape[0]
    out = dot(jnp.concatenate(a, axis=0), b[0])
    return out[:rows] + out[rows:] + dot(a[0], b[1])


def core():
    return lax.rem(lax.axis_index("tgt"), 2)


def rank_of(place):
    y, z = place // Z, place % Z
    return (y + AHEAD[0]) % (PLANE // Z) * Z + (z + AHEAD[1]) % Z


def owners(drug_devices, target_devices):
    places = sorted(range(drug_devices // 2), key=rank_of)
    return [
        [(2 * place + (low ^ block // 2)) * target_devices + block for low in range(2) for place in places]
        for block in range(target_devices)
    ]


def owned():
    place, block = lax.axis_index("cmp"), lax.axis_index("tgt")
    return (lax.rem(place, 2) ^ (block // 2)) * PLANE + rank_of(place // 2)


def eigen(drug_values, first, rows):
    rank = drug_values.shape[1]
    lane = lax.broadcasted_iota(jnp.int32, (rows, rank), 1)
    row = lax.broadcasted_iota(jnp.int32, (rows, rank), 0)
    return jnp.where(lane == row + first, drug_values[...], 0.0).sum(axis=1, keepdims=True)


def project(drug_basis, activity, out, basis, values, sems):
    devices, share, width = out.shape
    copies = [
        pltpu.make_async_copy(drug_basis, basis, sems.at[0]),
        pltpu.make_async_copy(activity, values, sems.at[1]),
    ]
    for copy in copies:
        copy.start()
    for copy in copies:
        copy.wait()
    sums = dot(basis[...], values[...], (0, 0))
    out[...] = sums.reshape(devices, share, width)


def forward(parts, target_basis, out, turned):
    out[...] = dot_halves(parts[...].sum(axis=0), target_basis[...])

    @pl.when(core() == 1)
    def _():
        turned[...] = target_basis[...].T


def middle(mine, other, target_basis, out, turned):
    out[...] = mine[...] + other[...]

    @pl.when(core() == 0)
    def _():
        turned[...] = target_basis[...].T


def of_core(work, turned_0, turned_1):
    @pl.when(core() == 0)
    def _():
        work(turned_0)

    @pl.when(core() == 1)
    def _():
        work(turned_1)


def leverage(drug_values, target_values, ridge, drug_basis, turned, pieces):
    wide = drug_basis[...].astype(jnp.float32)
    squares = halves(wide * wide)
    own = eigen(drug_values, 0, drug_values.shape[1])
    step = target_values.shape[1] // PIECES
    total = None
    for piece in pieces:
        some = slice(piece * step, (piece + 1) * step)
        product = own * target_values[:, some]
        mixed = dot_pairs(squares, halves(product / (product + ridge[0])))
        wide = turned[some].astype(jnp.float32)
        term = dot_pairs(halves(mixed), halves(wide * wide))
        total = term if total is None else total + term
    return total


def lever(drug_values, target_values, ridge, drug_basis, turned_0, turned_1, total, weights):
    values = drug_values, target_values, ridge, drug_basis
    product = eigen(drug_values, owned() * weights.shape[0], weights.shape[0]) * target_values[...]
    weights[...] = product / (product + ridge[0])

    @pl.when(core() == 0)
    def _():
        total[...] = leverage(*values, turned_0, range(PIECES))

    @pl.when(core() == 1)
    def _():
        total[...] = leverage(*values, turned_1, range(PIECES - LATE))


def backward(mine, other, weights, turned_0, turned_1, out):
    filtered = weights[...] * (mine[...] + other[...])

    def work(turned):
        out[...] = jnp.broadcast_to(dot_halves(filtered, turned[...])[None], out.shape)

    of_core(work, turned_0, turned_1)


def fit(parts, activity, total, drug_values, target_values, ridge, drug_basis, turned_1, fitted, residual, rest):
    devices, share, width = parts.shape
    rest[...] = total[...]

    @pl.when(core() == 1)
    def _():
        late = range(PIECES - LATE, PIECES)
        rest[...] += leverage(drug_values, target_values, ridge, drug_basis, turned_1, late)

    high, low = halves(parts[...].reshape(devices * share, width))
    basis = drug_basis[...]
    full = dot(basis, high) + dot(basis, low)
    fitted[...] = full.astype(fitted.dtype)
    wide = activity[...].astype(jnp.float32)
    residual[...] = ((wide - full) / (1.0 - rest[...])).astype(residual.dtype)


def call(body, outs, flops, scratch=(), far=(), scalar=()):
    def run(*args):
        vmem = pl.BlockSpec(memory_space=pltpu.VMEM)
        spaces = {**dict.fromkeys(far, pl.ANY), **dict.fromkeys(scalar, pltpu.SMEM)}
        return pl.pallas_call(
            body,
            out_shape=outs,
            in_specs=[pl.BlockSpec(memory_space=spaces.get(i, pltpu.VMEM)) for i in range(len(args))],
            out_specs=jax.tree.map(lambda _: vmem, outs),
            scratch_shapes=list(scratch),
            compiler_params=pltpu.CompilerParams(vmem_limit_bytes=40 * MIB),
            cost_estimate=pl.CostEstimate(
                flops=flops, bytes_accessed=sum(x.size * x.dtype.itemsize for x in args), transcendentals=0
            ),
            name=body.__name__,
        )(*args)

    return run


def shards(activity, drug_basis, target_basis, drug_values, target_values, ridge):
    drug_devices = lax.axis_size("cmp")
    target_devices = lax.axis_size("tgt")
    compounds, rank = drug_basis.shape
    targets_here, targets = target_basis.shape
    share = rank // drug_devices
    devices = range(drug_devices * target_devices)
    f32, bf16 = jnp.float32, jnp.bfloat16
    blocks = jax.ShapeDtypeStruct((drug_devices, share, targets_here), f32)
    rows = jax.ShapeDtypeStruct((share, targets), f32)
    here = jax.ShapeDtypeStruct((compounds, targets_here), f32)
    turned = jax.ShapeDtypeStruct((targets, targets_here), bf16)
    output = jax.ShapeDtypeStruct((compounds, targets_here), bf16)

    scratch = (
        pltpu.VMEM(drug_basis.shape, bf16),
        pltpu.VMEM(activity.shape, bf16),
        pltpu.SemaphoreType.DMA((2,)),
    )
    far = [pltpu.with_memory_space_constraint(x, pltpu.HBM) for x in (drug_basis, activity)]
    sums = call(project, blocks, 2 * compounds * rank * targets_here, scratch, far=(0, 1))(*far)
    groups = owners(drug_devices, target_devices)
    parts = lax.all_to_all(sums, ("cmp", "tgt"), 0, 0, axis_index_groups=groups)
    flops = 4 * share * targets_here * targets
    coeff, turned_1 = call(forward, (rows, turned), flops)(parts, target_basis)
    other = lax.ppermute(coeff, "tgt", [(i, i ^ 1) for i in range(target_devices)])
    coeff, turned_0 = call(middle, (rows, turned), targets_here * targets)(coeff, other, target_basis)
    across = target_devices | 2
    other = lax.ppermute(coeff, ("cmp", "tgt"), [(i, i ^ across) for i in devices])
    values = (drug_values[None], target_values[None], ridge, drug_basis)
    total, weights = call(lever, (here, rows), 6 * compounds * rank * targets, scalar=(2,))(
        *values, turned_0, turned_1
    )
    back = call(backward, blocks, flops)(coeff, other, weights, turned_0, turned_1)
    back = lax.all_to_all(back, ("cmp", "tgt"), 0, 0, axis_index_groups=groups)
    scratch = (pltpu.VMEM(here.shape, f32),)
    return call(fit, (output, output), 4 * compounds * rank * targets_here, scratch, scalar=(5,))(
        back, activity, total, *values, turned_1
    )


def solution(mesh):
    return jax.shard_map(
        shards,
        mesh=mesh,
        in_specs=(P("cmp", "tgt"), P("cmp", None), P("tgt", None), P(), P(), P()),
        out_specs=(P("cmp", "tgt"), P("cmp", "tgt")),
        check_vma=False,
    )
```

```python
import jax
import jax.numpy as jnp
from jax import lax
from jax.experimental import pallas as pl
from jax.experimental.pallas import tpu as pltpu
from jax.sharding import PartitionSpec as P

MIB = 1024 * 1024
PLANE, Z = 16, 4
AHEAD = (2, 1)
PIECES, LATE = 4, 2


def halves(x):
    high = x.astype(jnp.bfloat16)
    return high, (x - high.astype(jnp.float32)).astype(jnp.bfloat16)


def dot(a, b, along=(1, 0)):
    dims = (((along[0],), (along[1],)), ((), ()))
    return lax.dot_general(a, b, dims, preferred_element_type=jnp.float32)


def dot_halves(x, b):
    rows = x.shape[0]
    out = dot(jnp.concatenate(halves(x), axis=0), b)
    return out[:rows] + out[rows:]


def dot_pairs(a, b):
    rows = a[0].shape[0]
    out = dot(jnp.concatenate(a, axis=0), b[0])
    return out[:rows] + out[rows:] + dot(a[0], b[1])


def core():
    return lax.rem(lax.axis_index("tgt"), 2)


def rank_of(place):
    y, z = place // Z, place % Z
    return (y + AHEAD[0]) % (PLANE // Z) * Z + (z + AHEAD[1]) % Z


def owners(drug_devices, target_devices):
    places = sorted(range(drug_devices // 2), key=rank_of)
    return [
        [(2 * place + (low ^ block // 2)) * target_devices + block for low in range(2) for place in places]
        for block in range(target_devices)
    ]


def owned():
    place, block = lax.axis_index("cmp"), lax.axis_index("tgt")
    return (lax.rem(place, 2) ^ (block // 2)) * PLANE + rank_of(place // 2)


def eigen(drug_values, first, rows):
    rank = drug_values.shape[1]
    lane = lax.broadcasted_iota(jnp.int32, (rows, rank), 1)
    row = lax.broadcasted_iota(jnp.int32, (rows, rank), 0)
    return jnp.where(lane == row + first, drug_values[...], 0.0).sum(axis=1, keepdims=True)


def project(drug_basis, activity, out, basis, values, sems):
    devices, share, width = out.shape
    copies = [
        pltpu.make_async_copy(drug_basis, basis, sems.at[0]),
        pltpu.make_async_copy(activity, values, sems.at[1]),
    ]
    for copy in copies:
        copy.start()
    for copy in copies:
        copy.wait()
    sums = dot(basis[...], values[...], (0, 0))
    out[...] = sums.reshape(devices, share, width)


def forward(parts, target_basis, out, turned):
    out[...] = dot_halves(parts[...].sum(axis=0), target_basis[...])

    @pl.when(core() == 1)
    def _():
        turned[...] = target_basis[...].T


def middle(mine, other, target_basis, out, turned):
    out[...] = mine[...] + other[...]

    @pl.when(core() == 0)
    def _():
        turned[...] = target_basis[...].T


def of_core(work, turned_0, turned_1):
    @pl.when(core() == 0)
    def _():
        work(turned_0)

    @pl.when(core() == 1)
    def _():
        work(turned_1)


def leverage(drug_values, target_values, ridge, drug_basis, turned, pieces):
    wide = drug_basis[...].astype(jnp.float32)
    squares = halves(wide * wide)
    own = eigen(drug_values, 0, drug_values.shape[1])
    step = target_values.shape[1] // PIECES
    total = None
    for piece in pieces:
        some = slice(piece * step, (piece + 1) * step)
        product = own * target_values[:, some]
        mixed = dot_pairs(squares, halves(product / (product + ridge[0])))
        wide = turned[some].astype(jnp.float32)
        term = dot_pairs(halves(mixed), halves(wide * wide))
        total = term if total is None else total + term
    return total


def lever(drug_values, target_values, ridge, drug_basis, turned_0, turned_1, total, weights):
    values = drug_values, target_values, ridge, drug_basis
    product = eigen(drug_values, owned() * weights.shape[0], weights.shape[0]) * target_values[...]
    weights[...] = product / (product + ridge[0])

    @pl.when(core() == 0)
    def _():
        total[...] = leverage(*values, turned_0, range(PIECES))

    @pl.when(core() == 1)
    def _():
        total[...] = leverage(*values, turned_1, range(PIECES - LATE))


def backward(mine, other, weights, turned_0, turned_1, out):
    filtered = weights[...] * (mine[...] + other[...])

    def work(turned):
        out[...] = jnp.broadcast_to(dot_halves(filtered, turned[...])[None], out.shape)

    of_core(work, turned_0, turned_1)


def fit(parts, activity, total, drug_values, target_values, ridge, drug_basis, turned_1, fitted, residual, rest):
    devices, share, width = parts.shape
    rest[...] = total[...]

    @pl.when(core() == 1)
    def _():
        late = range(PIECES - LATE, PIECES)
        rest[...] += leverage(drug_values, target_values, ridge, drug_basis, turned_1, late)

    high, low = halves(parts[...].reshape(devices * share, width))
    basis = drug_basis[...]
    full = dot(basis, high) + dot(basis, low)
    fitted[...] = full.astype(fitted.dtype)
    wide = activity[...].astype(jnp.float32)
    residual[...] = ((wide - full) / (1.0 - rest[...])).astype(residual.dtype)


def call(body, outs, flops, scratch=(), far=(), scalar=()):
    def run(*args):
        vmem = pl.BlockSpec(memory_space=pltpu.VMEM)
        spaces = {**dict.fromkeys(far, pl.ANY), **dict.fromkeys(scalar, pltpu.SMEM)}
        return pl.pallas_call(
            body,
            out_shape=outs,
            in_specs=[pl.BlockSpec(memory_space=spaces.get(i, pltpu.VMEM)) for i in range(len(args))],
            out_specs=jax.tree.map(lambda _: vmem, outs),
            scratch_shapes=list(scratch),
            compiler_params=pltpu.CompilerParams(vmem_limit_bytes=40 * MIB),
            cost_estimate=pl.CostEstimate(
                flops=flops, bytes_accessed=sum(x.size * x.dtype.itemsize for x in args), transcendentals=0
            ),
            name=body.__name__,
        )(*args)

    return run


def shards(activity, drug_basis, target_basis, drug_values, target_values, ridge):
    drug_devices = lax.axis_size("cmp")
    target_devices = lax.axis_size("tgt")
    compounds, rank = drug_basis.shape
    targets_here, targets = target_basis.shape
    share = rank // drug_devices
    devices = range(drug_devices * target_devices)
    f32, bf16 = jnp.float32, jnp.bfloat16
    blocks = jax.ShapeDtypeStruct((drug_devices, share, targets_here), f32)
    rows = jax.ShapeDtypeStruct((share, targets), f32)
    here = jax.ShapeDtypeStruct((compounds, targets_here), f32)
    turned = jax.ShapeDtypeStruct((targets, targets_here), bf16)
    output = jax.ShapeDtypeStruct((compounds, targets_here), bf16)

    scratch = (
        pltpu.VMEM(drug_basis.shape, bf16),
        pltpu.VMEM(activity.shape, bf16),
        pltpu.SemaphoreType.DMA((2,)),
    )
    far = [pltpu.with_memory_space_constraint(x, pltpu.HBM) for x in (drug_basis, activity)]
    sums = call(project, blocks, 2 * compounds * rank * targets_here, scratch, far=(0, 1))(*far)
    groups = owners(drug_devices, target_devices)
    parts = lax.all_to_all(sums, ("cmp", "tgt"), 0, 0, axis_index_groups=groups)
    flops = 4 * share * targets_here * targets
    coeff, turned_1 = call(forward, (rows, turned), flops)(parts, target_basis)
    other = lax.ppermute(coeff, "tgt", [(i, i ^ 1) for i in range(target_devices)])
    coeff, turned_0 = call(middle, (rows, turned), targets_here * targets)(coeff, other, target_basis)
    across = target_devices | 2
    other = lax.ppermute(coeff, ("cmp", "tgt"), [(i, i ^ across) for i in devices])
    values = (drug_values[None], target_values[None], ridge, drug_basis)
    total, weights = call(lever, (here, rows), 6 * compounds * rank * targets, scalar=(2,))(
        *values, turned_0, turned_1
    )
    back = call(backward, blocks, flops)(coeff, other, weights, turned_0, turned_1)
    back = lax.all_to_all(back, ("cmp", "tgt"), 0, 0, axis_index_groups=groups)
    scratch = (pltpu.VMEM(here.shape, f32),)
    return call(fit, (output, output), 4 * compounds * rank * targets_here, scratch, scalar=(5,))(
        back, activity, total, *values, turned_1
    )


def solution(mesh):
    return jax.shard_map(
        shards,
        mesh=mesh,
        in_specs=(P("cmp", "tgt"), P("cmp", None), P("tgt", None), P(), P(), P()),
        out_specs=(P("cmp", "tgt"), P("cmp", "tgt")),
        check_vma=False,
    )
```

```python
import jax
import jax.numpy as jnp
from jax import lax
from jax.experimental import pallas as pl
from jax.experimental.pallas import tpu as pltpu
from jax.sharding import PartitionSpec as P

MIB = 1024 * 1024
PLANE, Z = 16, 4
AHEAD = (2, 1)
PIECES, LATE = 2, 1


def halves(x):
    high = x.astype(jnp.bfloat16)
    return high, (x - high.astype(jnp.float32)).astype(jnp.bfloat16)


def dot(a, b, along=(1, 0)):
    dims = (((along[0],), (along[1],)), ((), ()))
    return lax.dot_general(a, b, dims, preferred_element_type=jnp.float32)


def dot_halves(x, b):
    rows = x.shape[0]
    out = dot(jnp.concatenate(halves(x), axis=0), b)
    return out[:rows] + out[rows:]


def dot_pairs(a, b):
    rows = a[0].shape[0]
    out = dot(jnp.concatenate(a, axis=0), b[0])
    return out[:rows] + out[rows:] + dot(a[0], b[1])


def core():
    return lax.rem(lax.axis_index("tgt"), 2)


def rank_of(place):
    y, z = place // Z, place % Z
    return (y + AHEAD[0]) % (PLANE // Z) * Z + (z + AHEAD[1]) % Z


def owners(drug_devices, target_devices):
    places = sorted(range(drug_devices // 2), key=rank_of)
    return [
        [(2 * place + (low ^ block // 2)) * target_devices + block for low in range(2) for place in places]
        for block in range(target_devices)
    ]


def owned():
    place, block = lax.axis_index("cmp"), lax.axis_index("tgt")
    return (lax.rem(place, 2) ^ (block // 2)) * PLANE + rank_of(place // 2)


def eigen(drug_values, first, rows):
    rank = drug_values.shape[1]
    lane = lax.broadcasted_iota(jnp.int32, (rows, rank), 1)
    row = lax.broadcasted_iota(jnp.int32, (rows, rank), 0)
    return jnp.where(lane == row + first, drug_values[...], 0.0).sum(axis=1, keepdims=True)


def project(drug_basis, activity, out, basis, values, sems):
    devices, share, width = out.shape
    copies = [
        pltpu.make_async_copy(drug_basis, basis, sems.at[0]),
        pltpu.make_async_copy(activity, values, sems.at[1]),
    ]
    for copy in copies:
        copy.start()
    for copy in copies:
        copy.wait()
    sums = dot(basis[...], values[...], (0, 0))
    out[...] = sums.reshape(devices, share, width)


def forward(parts, target_basis, out, turned):
    out[...] = dot_halves(parts[...].sum(axis=0), target_basis[...])

    @pl.when(core() == 1)
    def _():
        turned[...] = target_basis[...].T


def middle(mine, other, target_basis, out, turned):
    out[...] = mine[...] + other[...]

    @pl.when(core() == 0)
    def _():
        turned[...] = target_basis[...].T


def of_core(work, turned_0, turned_1):
    @pl.when(core() == 0)
    def _():
        work(turned_0)

    @pl.when(core() == 1)
    def _():
        work(turned_1)


def leverage(drug_values, target_values, ridge, drug_basis, turned, pieces):
    wide = drug_basis[...].astype(jnp.float32)
    squares = halves(wide * wide)
    own = eigen(drug_values, 0, drug_values.shape[1])
    step = target_values.shape[1] // PIECES
    total = None
    for piece in pieces:
        some = slice(piece * step, (piece + 1) * step)
        product = own * target_values[:, some]
        mixed = dot_pairs(squares, halves(product / (product + ridge[0])))
        wide = turned[some].astype(jnp.float32)
        term = dot_pairs(halves(mixed), halves(wide * wide))
        total = term if total is None else total + term
    return total


def lever(drug_values, target_values, ridge, drug_basis, turned_0, turned_1, total, weights):
    values = drug_values, target_values, ridge, drug_basis
    product = eigen(drug_values, owned() * weights.shape[0], weights.shape[0]) * target_values[...]
    weights[...] = product / (product + ridge[0])

    @pl.when(core() == 0)
    def _():
        total[...] = leverage(*values, turned_0, range(PIECES))

    @pl.when(core() == 1)
    def _():
        total[...] = leverage(*values, turned_1, range(PIECES - LATE))


def backward(mine, other, weights, turned_0, turned_1, out):
    filtered = weights[...] * (mine[...] + other[...])

    def work(turned):
        out[...] = jnp.broadcast_to(dot_halves(filtered, turned[...])[None], out.shape)

    of_core(work, turned_0, turned_1)


def fit(parts, activity, total, drug_values, target_values, ridge, drug_basis, turned_1, fitted, residual, rest):
    devices, share, width = parts.shape
    rest[...] = total[...]

    @pl.when(core() == 1)
    def _():
        late = range(PIECES - LATE, PIECES)
        rest[...] += leverage(drug_values, target_values, ridge, drug_basis, turned_1, late)

    high, low = halves(parts[...].reshape(devices * share, width))
    basis = drug_basis[...]
    full = dot(basis, high) + dot(basis, low)
    fitted[...] = full.astype(fitted.dtype)
    wide = activity[...].astype(jnp.float32)
    residual[...] = ((wide - full) / (1.0 - rest[...])).astype(residual.dtype)


def call(body, outs, flops, scratch=(), far=(), scalar=()):
    def run(*args):
        vmem = pl.BlockSpec(memory_space=pltpu.VMEM)
        spaces = {**dict.fromkeys(far, pl.ANY), **dict.fromkeys(scalar, pltpu.SMEM)}
        return pl.pallas_call(
            body,
            out_shape=outs,
            in_specs=[pl.BlockSpec(memory_space=spaces.get(i, pltpu.VMEM)) for i in range(len(args))],
            out_specs=jax.tree.map(lambda _: vmem, outs),
            scratch_shapes=list(scratch),
            compiler_params=pltpu.CompilerParams(vmem_limit_bytes=40 * MIB),
            cost_estimate=pl.CostEstimate(
                flops=flops, bytes_accessed=sum(x.size * x.dtype.itemsize for x in args), transcendentals=0
            ),
            name=body.__name__,
        )(*args)

    return run


def shards(activity, drug_basis, target_basis, drug_values, target_values, ridge):
    drug_devices = lax.axis_size("cmp")
    target_devices = lax.axis_size("tgt")
    compounds, rank = drug_basis.shape
    targets_here, targets = target_basis.shape
    share = rank // drug_devices
    devices = range(drug_devices * target_devices)
    f32, bf16 = jnp.float32, jnp.bfloat16
    blocks = jax.ShapeDtypeStruct((drug_devices, share, targets_here), f32)
    rows = jax.ShapeDtypeStruct((share, targets), f32)
    here = jax.ShapeDtypeStruct((compounds, targets_here), f32)
    turned = jax.ShapeDtypeStruct((targets, targets_here), bf16)
    output = jax.ShapeDtypeStruct((compounds, targets_here), bf16)

    scratch = (
        pltpu.VMEM(drug_basis.shape, bf16),
        pltpu.VMEM(activity.shape, bf16),
        pltpu.SemaphoreType.DMA((2,)),
    )
    far = [pltpu.with_memory_space_constraint(x, pltpu.HBM) for x in (drug_basis, activity)]
    sums = call(project, blocks, 2 * compounds * rank * targets_here, scratch, far=(0, 1))(*far)
    groups = owners(drug_devices, target_devices)
    parts = lax.all_to_all(sums, ("cmp", "tgt"), 0, 0, axis_index_groups=groups)
    flops = 4 * share * targets_here * targets
    coeff, turned_1 = call(forward, (rows, turned), flops)(parts, target_basis)
    other = lax.ppermute(coeff, "tgt", [(i, i ^ 1) for i in range(target_devices)])
    coeff, turned_0 = call(middle, (rows, turned), targets_here * targets)(coeff, other, target_basis)
    across = target_devices | 2
    other = lax.ppermute(coeff, ("cmp", "tgt"), [(i, i ^ across) for i in devices])
    values = (drug_values[None], target_values[None], ridge, drug_basis)
    total, weights = call(lever, (here, rows), 6 * compounds * rank * targets, scalar=(2,))(
        *values, turned_0, turned_1
    )
    back = call(backward, blocks, flops)(coeff, other, weights, turned_0, turned_1)
    back = lax.all_to_all(back, ("cmp", "tgt"), 0, 0, axis_index_groups=groups)
    scratch = (pltpu.VMEM(here.shape, f32),)
    return call(fit, (output, output), 4 * compounds * rank * targets_here, scratch, scalar=(5,))(
        back, activity, total, *values, turned_1
    )


def solution(mesh):
    return jax.shard_map(
        shards,
        mesh=mesh,
        in_specs=(P("cmp", "tgt"), P("cmp", None), P("tgt", None), P(), P(), P()),
        out_specs=(P("cmp", "tgt"), P("cmp", "tgt")),
        check_vma=False,
    )
```

```python
import jax
import jax.numpy as jnp
from jax import lax
from jax.experimental import pallas as pl
from jax.experimental.pallas import tpu as pltpu
from jax.sharding import PartitionSpec as P

MIB = 1024 * 1024
PLANE, Z = 16, 4
AHEAD = (2, 3)
PIECES, LATE = 4, 2


def halves(x):
    high = x.astype(jnp.bfloat16)
    return high, (x - high.astype(jnp.float32)).astype(jnp.bfloat16)


def dot(a, b, along=(1, 0)):
    dims = (((along[0],), (along[1],)), ((), ()))
    return lax.dot_general(a, b, dims, preferred_element_type=jnp.float32)


def dot_halves(x, b):
    rows = x.shape[0]
    out = dot(jnp.concatenate(halves(x), axis=0), b)
    return out[:rows] + out[rows:]


def dot_pairs(a, b):
    rows = a[0].shape[0]
    out = dot(jnp.concatenate(a, axis=0), b[0])
    return out[:rows] + out[rows:] + dot(a[0], b[1])


def core():
    return lax.rem(lax.axis_index("tgt"), 2)


def rank_of(place):
    y, z = place // Z, place % Z
    return (AHEAD[0] - y) % (PLANE // Z) * Z + (AHEAD[1] - z) % Z


def owners(drug_devices, target_devices):
    places = sorted(range(drug_devices // 2), key=rank_of)
    return [
        [(2 * place + (low ^ block // 2)) * target_devices + block for low in range(2) for place in places]
        for block in range(target_devices)
    ]


def owned():
    place, block = lax.axis_index("cmp"), lax.axis_index("tgt")
    return (lax.rem(place, 2) ^ (block // 2)) * PLANE + rank_of(place // 2)


def eigen(drug_values, first, rows):
    rank = drug_values.shape[1]
    lane = lax.broadcasted_iota(jnp.int32, (rows, rank), 1)
    row = lax.broadcasted_iota(jnp.int32, (rows, rank), 0)
    return jnp.where(lane == row + first, drug_values[...], 0.0).sum(axis=1, keepdims=True)


def project(drug_basis, activity, out, basis, values, sems):
    devices, share, width = out.shape
    copies = [
        pltpu.make_async_copy(drug_basis, basis, sems.at[0]),
        pltpu.make_async_copy(activity, values, sems.at[1]),
    ]
    for copy in copies:
        copy.start()
    for copy in copies:
        copy.wait()
    sums = dot(basis[...], values[...], (0, 0))
    out[...] = sums.reshape(devices, share, width)


def forward(parts, target_basis, out, turned):
    out[...] = dot_halves(parts[...].sum(axis=0), target_basis[...])

    @pl.when(core() == 1)
    def _():
        turned[...] = target_basis[...].T


def middle(mine, other, target_basis, out, turned):
    out[...] = mine[...] + other[...]

    @pl.when(core() == 0)
    def _():
        turned[...] = target_basis[...].T


def of_core(work, turned_0, turned_1):
    @pl.when(core() == 0)
    def _():
        work(turned_0)

    @pl.when(core() == 1)
    def _():
        work(turned_1)


def leverage(drug_values, target_values, ridge, drug_basis, turned, pieces):
    wide = drug_basis[...].astype(jnp.float32)
    squares = halves(wide * wide)
    own = eigen(drug_values, 0, drug_values.shape[1])
    step = target_values.shape[1] // PIECES
    total = None
    for piece in pieces:
        some = slice(piece * step, (piece + 1) * step)
        product = own * target_values[:, some]
        mixed = dot_pairs(squares, halves(product / (product + ridge[0])))
        wide = turned[some].astype(jnp.float32)
        term = dot_pairs(halves(mixed), halves(wide * wide))
        total = term if total is None else total + term
    return total


def lever(drug_values, target_values, ridge, drug_basis, turned_0, turned_1, total, weights):
    values = drug_values, target_values, ridge, drug_basis
    product = eigen(drug_values, owned() * weights.shape[0], weights.shape[0]) * target_values[...]
    weights[...] = product / (product + ridge[0])

    @pl.when(core() == 0)
    def _():
        total[...] = leverage(*values, turned_0, range(PIECES))

    @pl.when(core() == 1)
    def _():
        total[...] = leverage(*values, turned_1, range(PIECES - LATE))


def backward(mine, other, weights, turned_0, turned_1, out):
    filtered = weights[...] * (mine[...] + other[...])

    def work(turned):
        out[...] = jnp.broadcast_to(dot_halves(filtered, turned[...])[None], out.shape)

    of_core(work, turned_0, turned_1)


def fit(parts, activity, total, drug_values, target_values, ridge, drug_basis, turned_1, fitted, residual, rest):
    devices, share, width = parts.shape
    rest[...] = total[...]

    @pl.when(core() == 1)
    def _():
        late = range(PIECES - LATE, PIECES)
        rest[...] += leverage(drug_values, target_values, ridge, drug_basis, turned_1, late)

    high, low = halves(parts[...].reshape(devices * share, width))
    basis = drug_basis[...]
    full = dot(basis, high) + dot(basis, low)
    fitted[...] = full.astype(fitted.dtype)
    wide = activity[...].astype(jnp.float32)
    residual[...] = ((wide - full) / (1.0 - rest[...])).astype(residual.dtype)


def call(body, outs, flops, scratch=(), far=(), scalar=()):
    def run(*args):
        vmem = pl.BlockSpec(memory_space=pltpu.VMEM)
        spaces = {**dict.fromkeys(far, pl.ANY), **dict.fromkeys(scalar, pltpu.SMEM)}
        return pl.pallas_call(
            body,
            out_shape=outs,
            in_specs=[pl.BlockSpec(memory_space=spaces.get(i, pltpu.VMEM)) for i in range(len(args))],
            out_specs=jax.tree.map(lambda _: vmem, outs),
            scratch_shapes=list(scratch),
            compiler_params=pltpu.CompilerParams(vmem_limit_bytes=40 * MIB),
            cost_estimate=pl.CostEstimate(
                flops=flops, bytes_accessed=sum(x.size * x.dtype.itemsize for x in args), transcendentals=0
            ),
            name=body.__name__,
        )(*args)

    return run


def shards(activity, drug_basis, target_basis, drug_values, target_values, ridge):
    drug_devices = lax.axis_size("cmp")
    target_devices = lax.axis_size("tgt")
    compounds, rank = drug_basis.shape
    targets_here, targets = target_basis.shape
    share = rank // drug_devices
    devices = range(drug_devices * target_devices)
    f32, bf16 = jnp.float32, jnp.bfloat16
    blocks = jax.ShapeDtypeStruct((drug_devices, share, targets_here), f32)
    rows = jax.ShapeDtypeStruct((share, targets), f32)
    here = jax.ShapeDtypeStruct((compounds, targets_here), f32)
    turned = jax.ShapeDtypeStruct((targets, targets_here), bf16)
    output = jax.ShapeDtypeStruct((compounds, targets_here), bf16)

    scratch = (
        pltpu.VMEM(drug_basis.shape, bf16),
        pltpu.VMEM(activity.shape, bf16),
        pltpu.SemaphoreType.DMA((2,)),
    )
    far = [pltpu.with_memory_space_constraint(x, pltpu.HBM) for x in (drug_basis, activity)]
    sums = call(project, blocks, 2 * compounds * rank * targets_here, scratch, far=(0, 1))(*far)
    groups = owners(drug_devices, target_devices)
    parts = lax.all_to_all(sums, ("cmp", "tgt"), 0, 0, axis_index_groups=groups)
    flops = 4 * share * targets_here * targets
    coeff, turned_1 = call(forward, (rows, turned), flops)(parts, target_basis)
    other = lax.ppermute(coeff, "tgt", [(i, i ^ 1) for i in range(target_devices)])
    coeff, turned_0 = call(middle, (rows, turned), targets_here * targets)(coeff, other, target_basis)
    across = target_devices | 2
    other = lax.ppermute(coeff, ("cmp", "tgt"), [(i, i ^ across) for i in devices])
    values = (drug_values[None], target_values[None], ridge, drug_basis)
    total, weights = call(lever, (here, rows), 6 * compounds * rank * targets, scalar=(2,))(
        *values, turned_0, turned_1
    )
    back = call(backward, blocks, flops)(coeff, other, weights, turned_0, turned_1)
    back = lax.all_to_all(back, ("cmp", "tgt"), 0, 0, axis_index_groups=groups)
    scratch = (pltpu.VMEM(here.shape, f32),)
    return call(fit, (output, output), 4 * compounds * rank * targets_here, scratch, scalar=(5,))(
        back, activity, total, *values, turned_1
    )


def solution(mesh):
    return jax.shard_map(
        shards,
        mesh=mesh,
        in_specs=(P("cmp", "tgt"), P("cmp", None), P("tgt", None), P(), P(), P()),
        out_specs=(P("cmp", "tgt"), P("cmp", "tgt")),
        check_vma=False,
    )
```

```python
import jax
import jax.numpy as jnp
from jax import lax
from jax.experimental import pallas as pl
from jax.experimental.pallas import tpu as pltpu
from jax.sharding import PartitionSpec as P

MIB = 1024 * 1024
PLANE, Z = 16, 4
AHEAD = (2, 3)
PIECES, LATE = 8, 3


def halves(x):
    high = x.astype(jnp.bfloat16)
    return high, (x - high.astype(jnp.float32)).astype(jnp.bfloat16)


def dot(a, b, along=(1, 0)):
    dims = (((along[0],), (along[1],)), ((), ()))
    return lax.dot_general(a, b, dims, preferred_element_type=jnp.float32)


def dot_halves(x, b):
    rows = x.shape[0]
    out = dot(jnp.concatenate(halves(x), axis=0), b)
    return out[:rows] + out[rows:]


def dot_pairs(a, b):
    rows = a[0].shape[0]
    out = dot(jnp.concatenate(a, axis=0), b[0])
    return out[:rows] + out[rows:] + dot(a[0], b[1])


def core():
    return lax.rem(lax.axis_index("tgt"), 2)


def rank_of(place):
    y, z = place // Z, place % Z
    return (AHEAD[0] - y) % (PLANE // Z) * Z + (AHEAD[1] - z) % Z


def owners(drug_devices, target_devices):
    places = sorted(range(drug_devices // 2), key=rank_of)
    return [
        [(2 * place + (low ^ block // 2)) * target_devices + block for low in range(2) for place in places]
        for block in range(target_devices)
    ]


def owned():
    place, block = lax.axis_index("cmp"), lax.axis_index("tgt")
    return (lax.rem(place, 2) ^ (block // 2)) * PLANE + rank_of(place // 2)


def eigen(drug_values, first, rows):
    rank = drug_values.shape[1]
    lane = lax.broadcasted_iota(jnp.int32, (rows, rank), 1)
    row = lax.broadcasted_iota(jnp.int32, (rows, rank), 0)
    return jnp.where(lane == row + first, drug_values[...], 0.0).sum(axis=1, keepdims=True)


def project(drug_basis, activity, out, basis, values, sems):
    devices, share, width = out.shape
    copies = [
        pltpu.make_async_copy(drug_basis, basis, sems.at[0]),
        pltpu.make_async_copy(activity, values, sems.at[1]),
    ]
    for copy in copies:
        copy.start()
    for copy in copies:
        copy.wait()
    sums = dot(basis[...], values[...], (0, 0))
    out[...] = sums.reshape(devices, share, width)


def forward(parts, target_basis, out, turned):
    out[...] = dot_halves(parts[...].sum(axis=0), target_basis[...])

    @pl.when(core() == 1)
    def _():
        turned[...] = target_basis[...].T


def middle(mine, other, target_basis, out, turned):
    out[...] = mine[...] + other[...]

    @pl.when(core() == 0)
    def _():
        turned[...] = target_basis[...].T


def of_core(work, turned_0, turned_1):
    @pl.when(core() == 0)
    def _():
        work(turned_0)

    @pl.when(core() == 1)
    def _():
        work(turned_1)


def leverage(drug_values, target_values, ridge, drug_basis, turned, pieces):
    wide = drug_basis[...].astype(jnp.float32)
    squares = halves(wide * wide)
    own = eigen(drug_values, 0, drug_values.shape[1])
    step = target_values.shape[1] // PIECES
    total = None
    for piece in pieces:
        some = slice(piece * step, (piece + 1) * step)
        product = own * target_values[:, some]
        mixed = dot_pairs(squares, halves(product / (product + ridge[0])))
        wide = turned[some].astype(jnp.float32)
        term = dot_pairs(halves(mixed), halves(wide * wide))
        total = term if total is None else total + term
    return total


def lever(drug_values, target_values, ridge, drug_basis, turned_0, turned_1, total, weights):
    values = drug_values, target_values, ridge, drug_basis
    product = eigen(drug_values, owned() * weights.shape[0], weights.shape[0]) * target_values[...]
    weights[...] = product / (product + ridge[0])

    @pl.when(core() == 0)
    def _():
        total[...] = leverage(*values, turned_0, range(PIECES))

    @pl.when(core() == 1)
    def _():
        total[...] = leverage(*values, turned_1, range(PIECES - LATE))


def backward(mine, other, weights, turned_0, turned_1, out):
    filtered = weights[...] * (mine[...] + other[...])

    def work(turned):
        out[...] = jnp.broadcast_to(dot_halves(filtered, turned[...])[None], out.shape)

    of_core(work, turned_0, turned_1)


def fit(parts, activity, total, drug_values, target_values, ridge, drug_basis, turned_1, fitted, residual, rest):
    devices, share, width = parts.shape
    rest[...] = total[...]

    @pl.when(core() == 1)
    def _():
        late = range(PIECES - LATE, PIECES)
        rest[...] += leverage(drug_values, target_values, ridge, drug_basis, turned_1, late)

    high, low = halves(parts[...].reshape(devices * share, width))
    basis = drug_basis[...]
    full = dot(basis, high) + dot(basis, low)
    fitted[...] = full.astype(fitted.dtype)
    wide = activity[...].astype(jnp.float32)
    residual[...] = ((wide - full) / (1.0 - rest[...])).astype(residual.dtype)


def call(body, outs, flops, scratch=(), far=(), scalar=()):
    def run(*args):
        vmem = pl.BlockSpec(memory_space=pltpu.VMEM)
        spaces = {**dict.fromkeys(far, pl.ANY), **dict.fromkeys(scalar, pltpu.SMEM)}
        return pl.pallas_call(
            body,
            out_shape=outs,
            in_specs=[pl.BlockSpec(memory_space=spaces.get(i, pltpu.VMEM)) for i in range(len(args))],
            out_specs=jax.tree.map(lambda _: vmem, outs),
            scratch_shapes=list(scratch),
            compiler_params=pltpu.CompilerParams(vmem_limit_bytes=40 * MIB),
            cost_estimate=pl.CostEstimate(
                flops=flops, bytes_accessed=sum(x.size * x.dtype.itemsize for x in args), transcendentals=0
            ),
            name=body.__name__,
        )(*args)

    return run


def shards(activity, drug_basis, target_basis, drug_values, target_values, ridge):
    drug_devices = lax.axis_size("cmp")
    target_devices = lax.axis_size("tgt")
    compounds, rank = drug_basis.shape
    targets_here, targets = target_basis.shape
    share = rank // drug_devices
    devices = range(drug_devices * target_devices)
    f32, bf16 = jnp.float32, jnp.bfloat16
    blocks = jax.ShapeDtypeStruct((drug_devices, share, targets_here), f32)
    rows = jax.ShapeDtypeStruct((share, targets), f32)
    here = jax.ShapeDtypeStruct((compounds, targets_here), f32)
    turned = jax.ShapeDtypeStruct((targets, targets_here), bf16)
    output = jax.ShapeDtypeStruct((compounds, targets_here), bf16)

    scratch = (
        pltpu.VMEM(drug_basis.shape, bf16),
        pltpu.VMEM(activity.shape, bf16),
        pltpu.SemaphoreType.DMA((2,)),
    )
    far = [pltpu.with_memory_space_constraint(x, pltpu.HBM) for x in (drug_basis, activity)]
    sums = call(project, blocks, 2 * compounds * rank * targets_here, scratch, far=(0, 1))(*far)
    groups = owners(drug_devices, target_devices)
    parts = lax.all_to_all(sums, ("cmp", "tgt"), 0, 0, axis_index_groups=groups)
    flops = 4 * share * targets_here * targets
    coeff, turned_1 = call(forward, (rows, turned), flops)(parts, target_basis)
    other = lax.ppermute(coeff, "tgt", [(i, i ^ 1) for i in range(target_devices)])
    coeff, turned_0 = call(middle, (rows, turned), targets_here * targets)(coeff, other, target_basis)
    across = target_devices | 2
    other = lax.ppermute(coeff, ("cmp", "tgt"), [(i, i ^ across) for i in devices])
    values = (drug_values[None], target_values[None], ridge, drug_basis)
    total, weights = call(lever, (here, rows), 6 * compounds * rank * targets, scalar=(2,))(
        *values, turned_0, turned_1
    )
    back = call(backward, blocks, flops)(coeff, other, weights, turned_0, turned_1)
    back = lax.all_to_all(back, ("cmp", "tgt"), 0, 0, axis_index_groups=groups)
    scratch = (pltpu.VMEM(here.shape, f32),)
    return call(fit, (output, output), 4 * compounds * rank * targets_here, scratch, scalar=(5,))(
        back, activity, total, *values, turned_1
    )


def solution(mesh):
    return jax.shard_map(
        shards,
        mesh=mesh,
        in_specs=(P("cmp", "tgt"), P("cmp", None), P("tgt", None), P(), P(), P()),
        out_specs=(P("cmp", "tgt"), P("cmp", "tgt")),
        check_vma=False,
    )
```
